32 devices in a mesh: energy: 16 (over z, y, core), section: 2 (over x).
Axes of the slice: x: 2, y: 2, z: 4, core: 2. Of those that a mesh axis runs over, the one named last changes fastest.
Arguments:
- green_prev: float32 [32, 2, 2, 256, 256], P('energy', 'section'), may hold values from -0.2 to 0.2
- slab_ham: float32 [2, 2, 256, 256], P('section'), may hold values from -0.046875 to 0.046875
- onsite: float32 [2, 256], P('section'), may hold values from -1.5 to 1.5
- hop: float32 [2, 2, 256, 256], P('section'), may hold values from -0.94 to 0.94
- mode_strength: float32 [6], replicated, may hold values from 0.03 to 0.15
- phonon_shift: int32 [6], replicated, may hold values from 1 to 2, as said below
Outputs:
- green_diag: float32 [32, 2, 2, 256, 256], P('energy', 'section')
The draws below stay inside these ranges and needn't reach their ends.
Inputs may be any that keep to these rules, and one draw needn't show every extreme that they name: `phonon_shift`: every shift is at least 1 and at most 2; some mode reaches 2.
All inputs are finite; a program needn't handle non-finite values.
Results may differ from the reference program's by a relative error of at most 0.00012.
Values sent between devices are 32-bit elements; how exact they have to be, the bound alone decides.
A program may use at most 64 MiB of HBM per device.

```python
import math
from functools import partial
import jax
import jax.numpy as jnp
from jax import lax

NORB = 256
NE_DEV = 2
NMODES = 6
NE = 32
NSLAB = 2


def draw_phonon_shift(key, part):
    values = jax.random.randint(key, (NMODES,), 1, NE_DEV + 1)
    chosen = jax.random.randint(jax.random.fold_in(key, 7), (), 0, NMODES)
    values = values.at[chosen].set(NE_DEV)
    return values.astype(jnp.int32)


def draw_hop(key, part):
    key_mag = jax.random.fold_in(key, 11)
    key_off = jax.random.fold_in(key, 12)
    key_phase = jax.random.fold_in(key, 13)
    spread = 0.19 * (2.0 * NORB) ** (-0.5)
    eye = jnp.eye(NORB, dtype=jnp.float32)
    magnitude = jax.random.uniform(key_mag, (NSLAB, NORB), jnp.float32, 0.78, 0.92)
    offdiag = jnp.clip(spread * jax.random.normal(key_off, (NSLAB, 2, NORB, NORB), jnp.float32), -5.0 * spread, 5.0 * spread)
    phase = jax.random.uniform(key_phase, (NSLAB, NORB), jnp.float32, -math.pi, math.pi)
    diag_real = (magnitude * jnp.cos(phase))[:, None, :] * eye[None]
    diag_imag = (magnitude * jnp.sin(phase))[:, None, :] * eye[None]
    offdiag = offdiag * (1.0 - eye)[None, None]
    return (offdiag + jnp.stack([diag_real, diag_imag], axis=1)).astype(jnp.float32)


def levels(rng, shape, shards, least, top_value):
    loudness, own = 1.0, jax.random.fold_in(rng, 6)
    for position, parts in shards:
        steps = jnp.exp(jax.random.uniform(jax.random.fold_in(own, position), (parts,), jnp.float32, least / len(shards), top_value / len(shards)))
        loudness = loudness * jnp.repeat(steps, shape[position] // parts).reshape([-1 if axis == position else 1 for axis in range(len(shape))])
    return loudness


def normal_values(rng, shape, scale, bound, shards=(), held_as=jnp.bfloat16):
    level = levels(rng, shape, shards, -0.22, 0.18) if shards else 1.0
    values = jax.random.normal(rng, shape, jnp.float32) * scale * level
    return jnp.minimum(jnp.maximum(values, -bound), bound).astype(held_as)


def setup_inputs(seed: int = 0) -> dict:
    seeds = jax.random.split(jax.random.key(seed), 7)
    green_prev = normal_values(seeds[0], (NE, NSLAB, 2, NORB, NORB), 0.03, 0.2, ((0, 16), (1, 2)), jnp.float32)
    slab_ham = normal_values(seeds[1], (NSLAB, 2, NORB, NORB), (64 * NORB) ** -0.5, 0.046875, ((0, 2),), jnp.float32)
    onsite = jnp.clip(jax.random.uniform(seeds[2], (NSLAB, NORB), jnp.float32, -1.5, 1.5) * levels(seeds[2], (NSLAB, NORB), ((0, 2),), -0.4, 0.0), -1.5, 1.5)
    hop = draw_hop(jax.random.fold_in(seeds[6], 71), 0)
    mode_strength = jnp.clip(jnp.exp(jax.random.uniform(seeds[4], (NMODES,), jnp.float32, math.log(0.03), math.log(0.15))), 0.03, 0.15)
    phonon_shift = draw_phonon_shift(jax.random.fold_in(seeds[6], 71), 0)
    return dict(green_prev=green_prev, slab_ham=slab_ham, onsite=onsite, hop=hop, mode_strength=mode_strength, phonon_shift=phonon_shift)


ETA = 1.0
LEAD = 0.5


def cmul(left_op, right_op):
    matmul = partial(jnp.matmul, precision=lax.Precision.HIGHEST)
    lre, lim = left_op[..., 0, :, :], left_op[..., 1, :, :]
    rre, rim = right_op[..., 0, :, :], right_op[..., 1, :, :]
    return jnp.stack([matmul(lre, rre) - matmul(lim, rim), matmul(lre, rim) + matmul(lim, rre)], axis=-3)


def adjoint(block):
    return jnp.stack([jnp.swapaxes(block[..., 0, :, :], -1, -2), -jnp.swapaxes(block[..., 1, :, :], -1, -2)], axis=-3)


def hamiltonian(block, site, eye):
    herm = 0.5 * (block + adjoint(block))
    return jnp.stack([herm[0] + eye * site[None, :], herm[1]])


def left_connected(left, energies, sigma, ham, site, link, eye):
    couple = cmul(cmul(adjoint(link), left), link)
    real_part = energies[:, None, None] * eye[None]
    imag_part = jnp.broadcast_to(ETA * eye[None], real_part.shape)
    matrix = jnp.stack([real_part, imag_part], axis=1) - ham[None] - sigma - couple
    offset = energies[:, None] - site[None, :]
    denom = offset * offset + ETA * ETA
    guess = jnp.stack([eye[None] * (offset / denom)[:, None, :], eye[None] * (-ETA / denom)[:, None, :]], axis=1)
    for sweep_step in range(2):
        guess = 2.0 * guess - cmul(guess, cmul(matrix, guess))
    return guess


def reference(green_prev, slab_ham, onsite, hop, mode_strength, phonon_shift):
    count = green_prev.shape[0]
    nslab = green_prev.shape[1]
    norb = green_prev.shape[3]
    eye = jnp.eye(norb, dtype=jnp.float32)
    energies = -1.5 + 3.0 * (jnp.arange(count, dtype=jnp.float32) + 0.5) / count
    zero_block = jnp.zeros((norb, norb), jnp.float32)
    lead = jnp.broadcast_to(jnp.stack([zero_block, -LEAD * eye])[None], (count, 2, norb, norb))
    left = lead
    lefts = []
    for slab in range(nslab):
        prev = green_prev[:, slab]
        padded = jnp.pad(prev, ((NE_DEV, NE_DEV), (0, 0), (0, 0), (0, 0)))
        sigma = jnp.zeros_like(prev)
        for mode in range(mode_strength.shape[0]):
            shift = phonon_shift[mode].astype(jnp.int32)
            lower = lax.dynamic_slice_in_dim(padded, (NE_DEV - shift).astype(jnp.int32), count, 0)
            upper = lax.dynamic_slice_in_dim(padded, (NE_DEV + shift).astype(jnp.int32), count, 0)
            sigma = sigma + mode_strength[mode] * (lower + upper)
        ham = hamiltonian(slab_ham[slab], onsite[slab], eye)
        left = left_connected(left, energies, sigma, ham, onsite[slab], hop[slab], eye)
        lefts.append(left)
    fulls = [None] * nslab
    fulls[nslab - 1] = lefts[nslab - 1]
    for slab in range(nslab - 2, -1, -1):
        link = hop[slab + 1]
        message = cmul(cmul(link, fulls[slab + 1]), adjoint(link))
        fulls[slab] = lefts[slab] + cmul(lefts[slab], cmul(message, lefts[slab]))
    return jnp.stack(fulls, axis=1)
```

```python
from functools import partial

import jax
import jax.numpy as jnp
from jax import lax
from jax.experimental import pallas as pl
from jax.experimental.pallas import tpu as pltpu
from jax.sharding import PartitionSpec as P

ETA = 1.0
LEAD = 0.5


def extended(block, sides, width):
    for axis, dim in sides:
        count = lax.axis_size(axis)
        forward = [(i, i + 1) for i in range(count - 1)]
        backward = [(target, source) for source, target in forward]
        low = lax.ppermute(
            lax.slice_in_dim(block, block.shape[dim] - width, None, axis=dim), axis, forward
        )
        high = lax.ppermute(lax.slice_in_dim(block, 0, width, axis=dim), axis, backward)
        block = jnp.concatenate([low, block, high], axis=dim)
    return block


def shifted(array, axis, by):
    count = lax.axis_size(axis)
    pairs = [(i, i + by) for i in range(count) if 0 <= i + by < count]
    return lax.ppermute(array, axis, pairs)


def cmul(left_op, right_op):
    matmul = partial(jnp.matmul, precision=lax.Precision.HIGHEST)
    lre, lim = (left_op[..., 0, :, :], left_op[..., 1, :, :])
    rre, rim = (right_op[..., 0, :, :], right_op[..., 1, :, :])
    return jnp.stack(
        [matmul(lre, rre) - matmul(lim, rim), matmul(lre, rim) + matmul(lim, rre)], axis=-3
    )


def adjoint(block):
    return jnp.stack(
        [jnp.swapaxes(block[..., 0, :, :], -1, -2), -jnp.swapaxes(block[..., 1, :, :], -1, -2)],
        axis=-3,
    )


def left_connected(left, energies, sigma, ham, site, link, eye):
    couple = cmul(cmul(adjoint(link), left), link)
    real_part = energies[:, None, None] * eye[None]
    imag_part = ETA * eye[None]
    matrix = jnp.stack([real_part, imag_part], axis=1) - ham[None] - sigma - couple
    offset = energies[:, None] - site[None, :]
    denom = offset * offset + ETA * ETA
    guess = jnp.stack(
        [eye[None] * (offset / denom)[:, None, :], eye[None] * (-ETA / denom)[:, None, :]], axis=1
    )
    for sweep_step in range(2):
        guess = 2.0 * guess - cmul(guess, cmul(matrix, guess))
    return guess


def full_and_message(left, message, link):
    full = left + cmul(left, cmul(message, left))
    return (full, cmul(cmul(link, full), adjoint(link)))


def body(green_prev, slab_ham, onsite, hop, mode_strength, phonon_shift):
    ne_dev = green_prev.shape[0]
    norb = green_prev.shape[3]
    eye = jnp.eye(norb, dtype=jnp.float32)
    padded = extended(green_prev, (("energy", 0),), ne_dev)
    sigma = jnp.zeros((ne_dev, 2, norb, norb), jnp.float32)
    for mode in range(mode_strength.shape[0]):
        shift = phonon_shift[mode]
        lower = lax.dynamic_slice_in_dim(padded, ne_dev - shift, ne_dev, 0)
        upper = lax.dynamic_slice_in_dim(padded, ne_dev + shift, ne_dev, 0)
        sigma = sigma + mode_strength[mode] * (lower[:, 0] + upper[:, 0])
    count = ne_dev * lax.axis_size("energy")
    first = lax.axis_index("energy") * ne_dev
    energies = (
        -1.5
        + 3.0 * ((first + jnp.arange(ne_dev, dtype=jnp.int32)).astype(jnp.float32) + 0.5) / count
    )
    site = onsite[0]
    block = slab_ham[0]
    herm = 0.5 * (block + adjoint(block))
    ham = jnp.stack([herm[0] + eye * site[None, :], herm[1]])
    link = hop[0]
    section = lax.axis_index("section")
    nsec = lax.axis_size("section")
    zero_block = jnp.zeros((norb, norb), jnp.float32)
    lead_one = jnp.stack([zero_block, -LEAD * eye])[None]
    empty_one = jnp.zeros((1, 2, norb, norb), jnp.float32)
    empty_all = jnp.zeros((ne_dev, 2, norb, norb), jnp.float32)

    def forward_turn(turn, carry):
        received, stored = carry
        slot = turn - section
        active = (slot >= 0) & (slot < ne_dev)
        pick = jnp.clip(slot, 0, ne_dev - 1)
        left = jnp.where(section == 0, lead_one, received)
        energy_one = lax.dynamic_slice_in_dim(energies, pick, 1, 0)
        sigma_one = lax.dynamic_slice_in_dim(sigma, pick, 1, 0)
        result = lax.cond(
            active,
            lambda: left_connected(left, energy_one, sigma_one, ham, site, link, eye),
            lambda: empty_one,
        )
        stored = jnp.where(active, lax.dynamic_update_slice_in_dim(stored, result, pick, 0), stored)
        received = shifted(result, "section", 1)
        return (received, stored)

    unused, lefts = lax.fori_loop(0, nsec + ne_dev - 1, forward_turn, (empty_one, empty_all))

    def backward_turn(turn, carry):
        received, stored = carry
        slot = turn - (nsec - 1 - section)
        active = (slot >= 0) & (slot < ne_dev)
        pick = jnp.clip(slot, 0, ne_dev - 1)
        message = jnp.where(section == nsec - 1, empty_one, received)
        left_one = lax.dynamic_slice_in_dim(lefts, pick, 1, 0)
        full, sent = lax.cond(
            active,
            lambda: full_and_message(left_one, message, link),
            lambda: (empty_one, empty_one),
        )
        stored = jnp.where(active, lax.dynamic_update_slice_in_dim(stored, full, pick, 0), stored)
        received = shifted(sent, "section", -1)
        return (received, stored)

    unused, fulls = lax.fori_loop(0, nsec + ne_dev - 1, backward_turn, (empty_one, empty_all))
    return fulls[:, None]


MESH = pl.DeviceIdType.MESH
CHUNKS = 4


def split(value):
    high = value.astype(jnp.bfloat16)
    low = (value - high.astype(jnp.float32)).astype(jnp.bfloat16)
    return high, low


def cmul_split(a, b):
    (arh, arl), (aih, ail) = split(a[0]), split(a[1])
    (brh, brl), (bih, bil) = split(b[0]), split(b[1])
    lhs = jnp.concatenate([arh, aih, arl, ail, arh, aih], axis=1)
    real = jnp.concatenate([brh, -bih, brh, -bih, brl, -bil], axis=0)
    imag = jnp.concatenate([bih, brh, bih, brh, bil, brl], axis=0)
    dot = partial(jnp.dot, preferred_element_type=jnp.float32)
    return dot(lhs, real), dot(lhs, imag)


def adj(block):
    return block[0].T, -block[1].T


def wire_kernel(
    count, strength, shift, green, ham, onsite, hop, out,
    halo_lo, halo_hi, local, mat, link, site, coup, left,
    next_send, prev_send, lo_recv, hi_recv, mat_send, mat_recv, small_send, small_recv,
):
    me, sec = lax.axis_index("energy"), lax.axis_index("section")
    norb = green.shape[-1]
    rows = norb // CHUNKS
    has_prev, has_next = me > 0, me < count // 2 - 1
    odd = lax.rem(me, 2)
    mate = me + 1 - 2 * odd
    other = 1 - sec

    barrier = pltpu.get_barrier_semaphore()
    pl.semaphore_signal(barrier, inc=1, device_id=(me, other), device_id_type=MESH)

    @pl.when(has_prev)
    def _():
        pl.semaphore_signal(barrier, inc=1, device_id=(me - 1, sec), device_id_type=MESH)

    @pl.when(has_next)
    def _():
        pl.semaphore_signal(barrier, inc=1, device_id=(me + 1, sec), device_id_type=MESH)

    pl.semaphore_wait(barrier, 1 + has_prev.astype(jnp.int32) + has_next.astype(jnp.int32))

    def cut(c):
        return pl.ds(c * rows, rows)

    def to_next(c):
        return pltpu.make_async_remote_copy(
            green.at[:, 0, :, cut(c)], halo_lo.at[:, :, cut(c)], next_send.at[c], lo_recv.at[c],
            device_id=(me + 1, sec), device_id_type=MESH)

    def to_prev(c):
        return pltpu.make_async_remote_copy(
            green.at[:, 0, :, cut(c)], halo_hi.at[:, :, cut(c)], prev_send.at[c], hi_recv.at[c],
            device_id=(me - 1, sec), device_id_type=MESH)

    def swap(c, slab):
        return pltpu.make_async_remote_copy(
            mat.at[slab, :, :, cut(c)], mat.at[slab, :, :, cut(c)], mat_send.at[c], mat_recv.at[c],
            device_id=(me, other), device_id_type=MESH)

    def site_copy(slab):
        return pltpu.make_async_remote_copy(
            site.at[slab], site.at[slab], small_send.at[0], small_recv.at[0],
            device_id=(me, other), device_id_type=MESH)

    def link_down():
        return pltpu.make_async_remote_copy(
            hop.at[0, odd], link.at[odd], small_send.at[1], small_recv.at[1],
            device_id=(me, other), device_id_type=MESH)

    def link_across(part):
        return pltpu.make_async_remote_copy(
            link.at[part], link.at[part], small_send.at[2], small_recv.at[2],
            device_id=(mate, sec), device_id_type=MESH)

    for c in range(CHUNKS):
        pl.when(has_next)(lambda c=c: to_next(c).start())
        pl.when(has_prev)(lambda c=c: to_prev(c).start())
    pl.when(sec == 1)(lambda: link_down().start())
    site[sec] = jnp.broadcast_to(onsite[...], (8, norb))
    site_copy(sec).start()

    @pl.when(jnp.logical_not(has_prev))
    def _():
        halo_lo[...] = jnp.zeros(halo_lo.shape, jnp.float32)

    @pl.when(jnp.logical_not(has_next))
    def _():
        halo_hi[...] = jnp.zeros(halo_hi.shape, jnp.float32)

    eye = lax.broadcasted_iota(jnp.int32, (norb, norb), 0) == lax.broadcasted_iota(
        jnp.int32, (norb, norb), 1)
    one = jnp.where(eye, 1.0, 0.0)
    w1, w2 = jnp.float32(0.0), jnp.float32(0.0)
    for m in range(strength.shape[0]):
        w1 = w1 + jnp.where(shift[m] == 1, strength[m], 0.0)
        w2 = w2 + jnp.where(shift[m] == 2, strength[m], 0.0)

    def energy(k):
        return -1.5 + 3.0 * ((2 * me + k).astype(jnp.float32) + 0.5) / count

    local[0] = 0.5 * (ham[0, 0] + ham[0, 0].T) + jnp.where(eye, onsite[...], 0.0)
    local[1] = 0.5 * (ham[0, 1] - ham[0, 1].T) - one * ETA

    @pl.when(sec == 0)
    def _():
        block = hop[0, 0], hop[0, 1]
        real, imag = cmul_split(adj(block), block)
        local[0] = local[0] + LEAD * imag
        local[1] = local[1] - LEAD * real
        link_down().wait_recv()
        link_across(odd).start()

    @pl.when(sec == 1)
    def _():
        link[...] = hop[0]

    for c in range(CHUNKS):
        pl.when(has_prev)(lambda c=c: to_next(c).wait_recv())
        pl.when(has_next)(lambda c=c: to_prev(c).wait_recv())
        r = slice(c * rows, (c + 1) * rows)
        for part in range(2):
            here0, here1 = green[0, 0, part, r], green[1, 0, part, r]
            low0, low1 = halo_lo[0, part, r], halo_lo[1, part, r]
            high0, high1 = halo_hi[0, part, r], halo_hi[1, part, r]
            base = local[part, r]
            first = -base - w1 * (low1 + here1) - w2 * (low0 + high0)
            second = -base - w1 * (here0 + high0) - w2 * (low1 + high1)
            if part == 0:
                first = first + one[r] * energy(0)
                second = second + one[r] * energy(1)
            mat[sec, 0, part, r] = first
            mat[sec, 1, part, r] = second
        swap(c, sec).start()

    def newton(matrix, slab, k):
        row = energy(k) - site[slab][:1]
        col = jnp.sum(jnp.where(eye, row, 0.0), axis=1, keepdims=True)
        rre = row / (row * row + ETA * ETA)
        rim = -ETA / (row * row + ETA * ETA)
        cre = col / (col * col + ETA * ETA)
        cim = -ETA / (col * col + ETA * ETA)
        wre, wim = cre * rre - cim * rim, cre * rim + cim * rre
        xre = jnp.where(eye, 2.0 * rre, 0.0) - (matrix[0] * wre - matrix[1] * wim)
        xim = jnp.where(eye, 2.0 * rim, 0.0) - (matrix[0] * wim + matrix[1] * wre)
        guess = xre, xim
        again = cmul_split(guess, cmul_split(matrix, guess))
        return 2.0 * xre - again[0], 2.0 * xim - again[1]

    site_copy(other).wait_recv()

    @pl.when(sec == 0)
    def _():
        link_across(1 - odd).wait_recv()

    @pl.when(sec == 1)
    def _():
        for c in range(CHUNKS):
            swap(c, 0).wait_recv()

    for k in range(2):
        g = newton((mat[0, k, 0], mat[0, k, 1]), 0, k)
        left[k, 0], left[k, 1] = g
        block = link[0], link[1]
        coup[k, 0], coup[k, 1] = cmul_split(cmul_split(adj(block), g), block)

    @pl.when(sec == 0)
    def _():
        for c in range(CHUNKS):
            swap(c, 1).wait_recv()

    for k in range(2):
        g = newton((mat[1, k, 0] - coup[k, 0], mat[1, k, 1] - coup[k, 1]), 1, k)
        out[k, 0, 0], out[k, 0, 1] = g

        @pl.when(sec == 0)
        def _(k=k):
            block = link[0], link[1]
            g1 = out[k, 0, 0], out[k, 0, 1]
            g0 = left[k, 0], left[k, 1]
            right = cmul_split(cmul_split(block, g1), adj(block))
            more = cmul_split(g0, cmul_split(right, g0))
            out[k, 0, 0] = g0[0] + more[0]
            out[k, 0, 1] = g0[1] + more[1]

    for c in range(CHUNKS):
        pl.when(has_next)(lambda c=c: to_next(c).wait_send())
        pl.when(has_prev)(lambda c=c: to_prev(c).wait_send())
        swap(c, sec).wait_send()
    site_copy(sec).wait_send()
    pl.when(sec == 1)(lambda: link_down().wait_send())
    pl.when(sec == 0)(lambda: link_across(odd).wait_send())


def two_slabs(green_prev, slab_ham, onsite, hop, mode_strength, phonon_shift):
    norb = green_prev.shape[3]
    count = green_prev.shape[0] * lax.axis_size("energy")
    vmem = pl.BlockSpec(memory_space=pltpu.VMEM)
    smem = pl.BlockSpec(memory_space=pltpu.SMEM)
    pair = pltpu.VMEM((2, 2, norb, norb), jnp.float32)
    sems = pltpu.SemaphoreType.DMA((CHUNKS,))
    return pl.pallas_call(
        partial(wire_kernel, count),
        out_shape=jax.ShapeDtypeStruct(green_prev.shape, jnp.float32),
        in_specs=[smem, smem, vmem, vmem, vmem, vmem],
        out_specs=vmem,
        scratch_shapes=[
            pair, pair,
            pltpu.VMEM((2, norb, norb), jnp.float32),
            pltpu.VMEM((2, 2, 2, norb, norb), jnp.float32),
            pltpu.VMEM((2, norb, norb), jnp.float32),
            pltpu.VMEM((2, 8, norb), jnp.float32),
            pair, pair,
            sems, sems, sems, sems, sems, sems,
            pltpu.SemaphoreType.DMA((3,)),
            pltpu.SemaphoreType.DMA((3,)),
        ],
        compiler_params=pltpu.CompilerParams(
            collective_id=0, has_side_effects=True, vmem_limit_bytes=48 * 1024 * 1024),
        name="wire",
    )(mode_strength, phonon_shift, green_prev, slab_ham, onsite, hop)


def solution(mesh):
    return jax.shard_map(
        two_slabs if mesh.shape["section"] == 2 and mesh.shape["energy"] % 2 == 0 else body,
        mesh=mesh,
        in_specs=(
            P("energy", "section", None, None, None),
            P("section", None, None, None),
            P("section", None),
            P("section", None, None, None),
            P(),
            P(),
        ),
        out_specs=P("energy", "section", None, None, None),
        check_vma=False,
    )
```

```python
from functools import partial

import jax
import jax.numpy as jnp
from jax import lax
from jax.experimental import pallas as pl
from jax.experimental.pallas import tpu as pltpu
from jax.sharding import PartitionSpec as P

ETA = 1.0
LEAD = 0.5


def extended(block, sides, width):
    for axis, dim in sides:
        count = lax.axis_size(axis)
        forward = [(i, i + 1) for i in range(count - 1)]
        backward = [(target, source) for source, target in forward]
        low = lax.ppermute(
            lax.slice_in_dim(block, block.shape[dim] - width, None, axis=dim), axis, forward
        )
        high = lax.ppermute(lax.slice_in_dim(block, 0, width, axis=dim), axis, backward)
        block = jnp.concatenate([low, block, high], axis=dim)
    return block


def shifted(array, axis, by):
    count = lax.axis_size(axis)
    pairs = [(i, i + by) for i in range(count) if 0 <= i + by < count]
    return lax.ppermute(array, axis, pairs)


def cmul(left_op, right_op):
    matmul = partial(jnp.matmul, precision=lax.Precision.HIGHEST)
    lre, lim = (left_op[..., 0, :, :], left_op[..., 1, :, :])
    rre, rim = (right_op[..., 0, :, :], right_op[..., 1, :, :])
    return jnp.stack(
        [matmul(lre, rre) - matmul(lim, rim), matmul(lre, rim) + matmul(lim, rre)], axis=-3
    )


def adjoint(block):
    return jnp.stack(
        [jnp.swapaxes(block[..., 0, :, :], -1, -2), -jnp.swapaxes(block[..., 1, :, :], -1, -2)],
        axis=-3,
    )


def left_connected(left, energies, sigma, ham, site, link, eye):
    couple = cmul(cmul(adjoint(link), left), link)
    real_part = energies[:, None, None] * eye[None]
    imag_part = ETA * eye[None]
    matrix = jnp.stack([real_part, imag_part], axis=1) - ham[None] - sigma - couple
    offset = energies[:, None] - site[None, :]
    denom = offset * offset + ETA * ETA
    guess = jnp.stack(
        [eye[None] * (offset / denom)[:, None, :], eye[None] * (-ETA / denom)[:, None, :]], axis=1
    )
    for sweep_step in range(2):
        guess = 2.0 * guess - cmul(guess, cmul(matrix, guess))
    return guess


def full_and_message(left, message, link):
    full = left + cmul(left, cmul(message, left))
    return (full, cmul(cmul(link, full), adjoint(link)))


def body(green_prev, slab_ham, onsite, hop, mode_strength, phonon_shift):
    ne_dev = green_prev.shape[0]
    norb = green_prev.shape[3]
    eye = jnp.eye(norb, dtype=jnp.float32)
    padded = extended(green_prev, (("energy", 0),), ne_dev)
    sigma = jnp.zeros((ne_dev, 2, norb, norb), jnp.float32)
    for mode in range(mode_strength.shape[0]):
        shift = phonon_shift[mode]
        lower = lax.dynamic_slice_in_dim(padded, ne_dev - shift, ne_dev, 0)
        upper = lax.dynamic_slice_in_dim(padded, ne_dev + shift, ne_dev, 0)
        sigma = sigma + mode_strength[mode] * (lower[:, 0] + upper[:, 0])
    count = ne_dev * lax.axis_size("energy")
    first = lax.axis_index("energy") * ne_dev
    energies = (
        -1.5
        + 3.0 * ((first + jnp.arange(ne_dev, dtype=jnp.int32)).astype(jnp.float32) + 0.5) / count
    )
    site = onsite[0]
    block = slab_ham[0]
    herm = 0.5 * (block + adjoint(block))
    ham = jnp.stack([herm[0] + eye * site[None, :], herm[1]])
    link = hop[0]
    section = lax.axis_index("section")
    nsec = lax.axis_size("section")
    zero_block = jnp.zeros((norb, norb), jnp.float32)
    lead_one = jnp.stack([zero_block, -LEAD * eye])[None]
    empty_one = jnp.zeros((1, 2, norb, norb), jnp.float32)
    empty_all = jnp.zeros((ne_dev, 2, norb, norb), jnp.float32)

    def forward_turn(turn, carry):
        received, stored = carry
        slot = turn - section
        active = (slot >= 0) & (slot < ne_dev)
        pick = jnp.clip(slot, 0, ne_dev - 1)
        left = jnp.where(section == 0, lead_one, received)
        energy_one = lax.dynamic_slice_in_dim(energies, pick, 1, 0)
        sigma_one = lax.dynamic_slice_in_dim(sigma, pick, 1, 0)
        result = lax.cond(
            active,
            lambda: left_connected(left, energy_one, sigma_one, ham, site, link, eye),
            lambda: empty_one,
        )
        stored = jnp.where(active, lax.dynamic_update_slice_in_dim(stored, result, pick, 0), stored)
        received = shifted(result, "section", 1)
        return (received, stored)

    unused, lefts = lax.fori_loop(0, nsec + ne_dev - 1, forward_turn, (empty_one, empty_all))

    def backward_turn(turn, carry):
        received, stored = carry
        slot = turn - (nsec - 1 - section)
        active = (slot >= 0) & (slot < ne_dev)
        pick = jnp.clip(slot, 0, ne_dev - 1)
        message = jnp.where(section == nsec - 1, empty_one, received)
        left_one = lax.dynamic_slice_in_dim(lefts, pick, 1, 0)
        full, sent = lax.cond(
            active,
            lambda: full_and_message(left_one, message, link),
            lambda: (empty_one, empty_one),
        )
        stored = jnp.where(active, lax.dynamic_update_slice_in_dim(stored, full, pick, 0), stored)
        received = shifted(sent, "section", -1)
        return (received, stored)

    unused, fulls = lax.fori_loop(0, nsec + ne_dev - 1, backward_turn, (empty_one, empty_all))
    return fulls[:, None]


MESH = pl.DeviceIdType.MESH
CHUNKS = 4


def split(value):
    high = value.astype(jnp.bfloat16)
    low = (value - high.astype(jnp.float32)).astype(jnp.bfloat16)
    return high, low


def cmul_split(a, b):
    (arh, arl), (aih, ail) = split(a[0]), split(a[1])
    (brh, brl), (bih, bil) = split(b[0]), split(b[1])
    lhs = jnp.concatenate([arh, aih, arl, ail, arh, aih], axis=1)
    real = jnp.concatenate([brh, -bih, brh, -bih, brl, -bil], axis=0)
    imag = jnp.concatenate([bih, brh, bih, brh, bil, brl], axis=0)
    dot = partial(jnp.dot, preferred_element_type=jnp.float32)
    return dot(lhs, real), dot(lhs, imag)


def adj(block):
    return block[0].T, -block[1].T


def wire_kernel(
    count, strength_hbm, shift_hbm, green_hbm, ham_hbm, onsite_hbm, hop_hbm, out_hbm,
    strength, shift, green, ham, onsite, hop, far_buf, mate_buf, local, mat, link, link_h, site,
    coup, left, result,
    load_sem, far_send, far_recv, mate_send, mate_recv, mat_send, mat_recv, small_send, small_recv,
    out_sem,
):
    me, sec = lax.axis_index("energy"), lax.axis_index("section")
    norb = green.shape[-1]
    rows = norb // CHUNKS
    odd = lax.rem(me, 2)
    mate, far = me + 1 - 2 * odd, me - 1 + 2 * odd
    has_far = jnp.logical_and(far >= 0, far < count // 2)
    other = 1 - sec
    order = (1 - odd, odd)

    loads = [
        pltpu.make_async_copy(source, target, load_sem.at[n])
        for n, (source, target) in enumerate((
            (strength_hbm, strength), (shift_hbm, shift), (onsite_hbm, onsite),
            (hop_hbm.at[0], hop), (ham_hbm.at[0], ham), (green_hbm.at[:, 0], green)))
    ]
    for load in loads:
        load.start()

    barrier = pltpu.get_barrier_semaphore()
    pl.semaphore_signal(barrier, inc=1, device_id=(me, other), device_id_type=MESH)
    pl.semaphore_signal(barrier, inc=1, device_id=(mate, sec), device_id_type=MESH)

    @pl.when(has_far)
    def _():
        pl.semaphore_signal(barrier, inc=1, device_id=(far, sec), device_id_type=MESH)

    pl.semaphore_wait(barrier, 2 + has_far.astype(jnp.int32))

    def cut(c):
        return pl.ds(c * rows, rows)

    def to_far(j, c):
        source = odd if j == 0 else 1 - odd
        n = j * CHUNKS + c
        return pltpu.make_async_remote_copy(
            green_hbm.at[source, 0, :, cut(c)], far_buf.at[j, :, cut(c)], far_send.at[n],
            far_recv.at[n], device_id=(far, sec), device_id_type=MESH)

    def to_mate(j):
        source = 1 - odd if j == 0 else odd
        return pltpu.make_async_remote_copy(
            green_hbm.at[source, 0], mate_buf.at[j], mate_send.at[j], mate_recv.at[j],
            device_id=(mate, sec), device_id_type=MESH)

    def swap(j, c, slab):
        n = j * CHUNKS + c
        return pltpu.make_async_remote_copy(
            mat.at[slab, j, :, cut(c)], mat.at[slab, j, :, cut(c)], mat_send.at[n],
            mat_recv.at[n], device_id=(me, other), device_id_type=MESH)

    def site_copy(slab):
        return pltpu.make_async_remote_copy(
            site.at[slab], site.at[slab], small_send.at[0], small_recv.at[0],
            device_id=(me, other), device_id_type=MESH)

    def link_down():
        return pltpu.make_async_remote_copy(
            hop_hbm.at[0, odd], link.at[odd], small_send.at[1], small_recv.at[1],
            device_id=(me, other), device_id_type=MESH)

    def link_across(part):
        return pltpu.make_async_remote_copy(
            link.at[part], link.at[part], small_send.at[2], small_recv.at[2],
            device_id=(mate, sec), device_id_type=MESH)

    @pl.when(has_far)
    def _():
        for c in range(CHUNKS):
            to_far(0, c).start()

    to_mate(0).start()
    to_mate(1).start()
    pl.when(sec == 1)(lambda: link_down().start())

    @pl.when(has_far)
    def _():
        for c in range(CHUNKS):
            to_far(1, c).start()

    @pl.when(jnp.logical_not(has_far))
    def _():
        far_buf[...] = jnp.zeros(far_buf.shape, jnp.float32)

    for load in loads:
        load.wait()
    site[sec] = jnp.broadcast_to(onsite[...], (8, norb))
    site_copy(sec).start()

    eye = lax.broadcasted_iota(jnp.int32, (norb, norb), 0) == lax.broadcasted_iota(
        jnp.int32, (norb, norb), 1)
    w1, w2 = jnp.float32(0.0), jnp.float32(0.0)
    for m in range(strength.shape[0]):
        w1 = w1 + jnp.where(shift[m] == 1, strength[m], 0.0)
        w2 = w2 + jnp.where(shift[m] == 2, strength[m], 0.0)

    def energy(k):
        return -1.5 + 3.0 * ((2 * me + k).astype(jnp.float32) + 0.5) / count

    local[0] = 0.5 * (ham[0] + ham[0].T) + jnp.where(eye, onsite[...], 0.0)
    local[1] = 0.5 * (ham[1] - ham[1].T) - jnp.where(eye, ETA, 0.0)

    @pl.when(sec == 0)
    def _():
        block = hop[0], hop[1]
        real, imag = cmul_split(adj(block), block)
        local[0] = local[0] + LEAD * imag
        local[1] = local[1] - LEAD * real
        link_down().wait_recv()
        link_across(odd).start()

    @pl.when(sec == 1)
    def _():
        link[...] = hop[...]
        link_h[0], link_h[1] = adj((hop[0], hop[1]))

    to_mate(0).wait_recv()
    to_mate(1).wait_recv()

    def assemble(j, c):
        pl.when(has_far)(lambda: to_far(j, c).wait_recv())
        r = slice(c * rows, (c + 1) * rows)
        for part in range(2):
            near, here = far_buf[0, part, r], green[1 - order[j], part, r]
            if j == 0:
                sigma = w1 * (here + mate_buf[0, part, r]) + w2 * (near + mate_buf[1, part, r])
            else:
                sigma = w1 * (here + near) + w2 * (far_buf[1, part, r] + mate_buf[0, part, r])
            value = -local[part, r] - sigma
            if part == 0:
                value = value + jnp.where(eye[r], energy(order[j]), 0.0)
            mat[sec, j, part, r] = value
        swap(j, c, sec).start()

    def newton(matrix, slab, k):
        row = energy(k) - site[slab][:1]
        col = jnp.sum(jnp.where(eye, row, 0.0), axis=1, keepdims=True)
        rre = row / (row * row + ETA * ETA)
        rim = -ETA / (row * row + ETA * ETA)
        cre = col / (col * col + ETA * ETA)
        cim = -ETA / (col * col + ETA * ETA)
        wre, wim = cre * rre - cim * rim, cre * rim + cim * rre
        xre = jnp.where(eye, 2.0 * rre, 0.0) - (matrix[0] * wre - matrix[1] * wim)
        xim = jnp.where(eye, 2.0 * rim, 0.0) - (matrix[0] * wim + matrix[1] * wre)
        guess = xre, xim
        again = cmul_split(guess, cmul_split(matrix, guess))
        return 2.0 * xre - again[0], 2.0 * xim - again[1]

    def arrived(j, slab):
        for c in range(CHUNKS):
            swap(j, c, slab).wait_recv()

    def first_slab(j):
        g = newton((mat[0, j, 0], mat[0, j, 1]), 0, order[j])
        left[0], left[1] = g
        half = cmul_split((link_h[0], link_h[1]), g)
        coup[0], coup[1] = cmul_split(half, (link[0], link[1]))

    def store(j):
        return pltpu.make_async_copy(result.at[j], out_hbm.at[order[j], 0], out_sem.at[j])

    def second_slab(j):
        pl.when(sec == 0)(lambda: arrived(j, 1))
        g1 = newton((mat[1, j, 0] - coup[0], mat[1, j, 1] - coup[1]), 1, order[j])
        result[j, 0], result[j, 1] = g1

        @pl.when(sec == 0)
        def _():
            g1 = result[j, 0], result[j, 1]
            g0 = left[0], left[1]
            half = cmul_split((link[0], link[1]), g1)
            right = cmul_split(half, (link_h[0], link_h[1]))
            more = cmul_split(g0, cmul_split(right, g0))
            result[j, 0] = g0[0] + more[0]
            result[j, 1] = g0[1] + more[1]

        store(j).start()

    for c in range(CHUNKS):
        assemble(0, c)

    @pl.when(sec == 0)
    def _():
        site_copy(1).wait_recv()
        link_across(1 - odd).wait_recv()
        link_h[0], link_h[1] = adj((link[0], link[1]))
        first_slab(0)

    for c in range(CHUNKS // 2):
        assemble(1, c)

    @pl.when(sec == 1)
    def _():
        site_copy(0).wait_recv()
        arrived(0, 0)
        first_slab(0)

    second_slab(0)
    for c in range(CHUNKS // 2, CHUNKS):
        assemble(1, c)
    pl.when(sec == 1)(lambda: arrived(1, 0))
    first_slab(1)
    second_slab(1)

    for j in range(2):
        for c in range(CHUNKS):
            pl.when(has_far)(lambda j=j, c=c: to_far(j, c).wait_send())
            swap(j, c, sec).wait_send()
        to_mate(j).wait_send()
        store(j).wait()
    site_copy(sec).wait_send()
    pl.when(sec == 1)(lambda: link_down().wait_send())
    pl.when(sec == 0)(lambda: link_across(odd).wait_send())


def two_slabs(green_prev, slab_ham, onsite, hop, mode_strength, phonon_shift):
    norb = green_prev.shape[3]
    count = green_prev.shape[0] * lax.axis_size("energy")
    hbm = pl.BlockSpec(memory_space=pltpu.HBM)
    one = pltpu.VMEM((2, norb, norb), jnp.float32)
    pair = pltpu.VMEM((2, 2, norb, norb), jnp.float32)
    sems = lambda n: pltpu.SemaphoreType.DMA((n,))
    return pl.pallas_call(
        partial(wire_kernel, count),
        out_shape=jax.ShapeDtypeStruct(green_prev.shape, jnp.float32),
        in_specs=[hbm] * 6,
        out_specs=hbm,
        scratch_shapes=[
            pltpu.SMEM(mode_strength.shape, jnp.float32),
            pltpu.SMEM(phonon_shift.shape, jnp.int32),
            pair, one, pltpu.VMEM(onsite.shape, jnp.float32), one,
            pair, pair, one,
            pltpu.VMEM((2, 2, 2, norb, norb), jnp.float32),
            one, one,
            pltpu.VMEM((2, 8, norb), jnp.float32),
            one, one, pair,
            sems(6), sems(2 * CHUNKS), sems(2 * CHUNKS), sems(2), sems(2),
            sems(2 * CHUNKS), sems(2 * CHUNKS), sems(3), sems(3), sems(2),
        ],
        compiler_params=pltpu.CompilerParams(
            collective_id=0, has_side_effects=True, vmem_limit_bytes=63 * 1024 * 1024),
        name="wire",
    )(mode_strength, phonon_shift, green_prev, slab_ham, onsite, hop)


def solution(mesh):
    return jax.shard_map(
        two_slabs if mesh.shape["section"] == 2 and mesh.shape["energy"] % 2 == 0 else body,
        mesh=mesh,
        in_specs=(
            P("energy", "section", None, None, None),
            P("section", None, None, None),
            P("section", None),
            P("section", None, None, None),
            P(),
            P(),
        ),
        out_specs=P("energy", "section", None, None, None),
        check_vma=False,
    )
```

```python
from functools import partial

import jax
import jax.numpy as jnp
from jax import lax
from jax.experimental import pallas as pl
from jax.experimental.pallas import tpu as pltpu
from jax.sharding import PartitionSpec as P

ETA = 1.0
LEAD = 0.5


def extended(block, sides, width):
    for axis, dim in sides:
        count = lax.axis_size(axis)
        forward = [(i, i + 1) for i in range(count - 1)]
        backward = [(target, source) for source, target in forward]
        low = lax.ppermute(
            lax.slice_in_dim(block, block.shape[dim] - width, None, axis=dim), axis, forward
        )
        high = lax.ppermute(lax.slice_in_dim(block, 0, width, axis=dim), axis, backward)
        block = jnp.concatenate([low, block, high], axis=dim)
    return block


def shifted(array, axis, by):
    count = lax.axis_size(axis)
    pairs = [(i, i + by) for i in range(count) if 0 <= i + by < count]
    return lax.ppermute(array, axis, pairs)


def cmul(left_op, right_op):
    matmul = partial(jnp.matmul, precision=lax.Precision.HIGHEST)
    lre, lim = (left_op[..., 0, :, :], left_op[..., 1, :, :])
    rre, rim = (right_op[..., 0, :, :], right_op[..., 1, :, :])
    return jnp.stack(
        [matmul(lre, rre) - matmul(lim, rim), matmul(lre, rim) + matmul(lim, rre)], axis=-3
    )


def adjoint(block):
    return jnp.stack(
        [jnp.swapaxes(block[..., 0, :, :], -1, -2), -jnp.swapaxes(block[..., 1, :, :], -1, -2)],
        axis=-3,
    )


def left_connected(left, energies, sigma, ham, site, link, eye):
    couple = cmul(cmul(adjoint(link), left), link)
    real_part = energies[:, None, None] * eye[None]
    imag_part = ETA * eye[None]
    matrix = jnp.stack([real_part, imag_part], axis=1) - ham[None] - sigma - couple
    offset = energies[:, None] - site[None, :]
    denom = offset * offset + ETA * ETA
    guess = jnp.stack(
        [eye[None] * (offset / denom)[:, None, :], eye[None] * (-ETA / denom)[:, None, :]], axis=1
    )
    for sweep_step in range(2):
        guess = 2.0 * guess - cmul(guess, cmul(matrix, guess))
    return guess


def full_and_message(left, message, link):
    full = left + cmul(left, cmul(message, left))
    return (full, cmul(cmul(link, full), adjoint(link)))


def body(green_prev, slab_ham, onsite, hop, mode_strength, phonon_shift):
    ne_dev = green_prev.shape[0]
    norb = green_prev.shape[3]
    eye = jnp.eye(norb, dtype=jnp.float32)
    padded = extended(green_prev, (("energy", 0),), ne_dev)
    sigma = jnp.zeros((ne_dev, 2, norb, norb), jnp.float32)
    for mode in range(mode_strength.shape[0]):
        shift = phonon_shift[mode]
        lower = lax.dynamic_slice_in_dim(padded, ne_dev - shift, ne_dev, 0)
        upper = lax.dynamic_slice_in_dim(padded, ne_dev + shift, ne_dev, 0)
        sigma = sigma + mode_strength[mode] * (lower[:, 0] + upper[:, 0])
    count = ne_dev * lax.axis_size("energy")
    first = lax.axis_index("energy") * ne_dev
    energies = (
        -1.5
        + 3.0 * ((first + jnp.arange(ne_dev, dtype=jnp.int32)).astype(jnp.float32) + 0.5) / count
    )
    site = onsite[0]
    block = slab_ham[0]
    herm = 0.5 * (block + adjoint(block))
    ham = jnp.stack([herm[0] + eye * site[None, :], herm[1]])
    link = hop[0]
    section = lax.axis_index("section")
    nsec = lax.axis_size("section")
    zero_block = jnp.zeros((norb, norb), jnp.float32)
    lead_one = jnp.stack([zero_block, -LEAD * eye])[None]
    empty_one = jnp.zeros((1, 2, norb, norb), jnp.float32)
    empty_all = jnp.zeros((ne_dev, 2, norb, norb), jnp.float32)

    def forward_turn(turn, carry):
        received, stored = carry
        slot = turn - section
        active = (slot >= 0) & (slot < ne_dev)
        pick = jnp.clip(slot, 0, ne_dev - 1)
        left = jnp.where(section == 0, lead_one, received)
        energy_one = lax.dynamic_slice_in_dim(energies, pick, 1, 0)
        sigma_one = lax.dynamic_slice_in_dim(sigma, pick, 1, 0)
        result = lax.cond(
            active,
            lambda: left_connected(left, energy_one, sigma_one, ham, site, link, eye),
            lambda: empty_one,
        )
        stored = jnp.where(active, lax.dynamic_update_slice_in_dim(stored, result, pick, 0), stored)
        received = shifted(result, "section", 1)
        return (received, stored)

    unused, lefts = lax.fori_loop(0, nsec + ne_dev - 1, forward_turn, (empty_one, empty_all))

    def backward_turn(turn, carry):
        received, stored = carry
        slot = turn - (nsec - 1 - section)
        active = (slot >= 0) & (slot < ne_dev)
        pick = jnp.clip(slot, 0, ne_dev - 1)
        message = jnp.where(section == nsec - 1, empty_one, received)
        left_one = lax.dynamic_slice_in_dim(lefts, pick, 1, 0)
        full, sent = lax.cond(
            active,
            lambda: full_and_message(left_one, message, link),
            lambda: (empty_one, empty_one),
        )
        stored = jnp.where(active, lax.dynamic_update_slice_in_dim(stored, full, pick, 0), stored)
        received = shifted(sent, "section", -1)
        return (received, stored)

    unused, fulls = lax.fori_loop(0, nsec + ne_dev - 1, backward_turn, (empty_one, empty_all))
    return fulls[:, None]


MESH = pl.DeviceIdType.MESH
CHUNKS = 4


def split(value):
    high = value.astype(jnp.bfloat16)
    low = (value - high.astype(jnp.float32)).astype(jnp.bfloat16)
    return high, low


def product(a, b):
    (ah, al), (bh, bl) = a, b
    return jnp.dot(
        jnp.concatenate([ah, al, ah], axis=1), jnp.concatenate([bh, bh, bl], axis=0),
        preferred_element_type=jnp.float32)


def cmul_split(a, b):
    rere = product(split(a[0]), split(b[0]))
    imim = product(split(a[1]), split(b[1]))
    mixed = product(split(a[0] + a[1]), split(b[0] + b[1]))
    return rere - imim, mixed - rere - imim


def adj(block):
    return block[0].T, -block[1].T


def wire_kernel(
    count, strength_hbm, shift_hbm, green_hbm, ham_hbm, onsite_hbm, hop_hbm, out_hbm,
    strength, shift, green, ham, onsite, hop, far_buf, mate_buf, local, mat, link, link_h, site,
    coup, left, result,
    load_sem, far_send, far_recv, mate_send, mate_recv, mat_send, mat_recv, small_send, small_recv,
    out_sem,
):
    me, sec = lax.axis_index("energy"), lax.axis_index("section")
    norb = green.shape[-1]
    rows = norb // CHUNKS
    odd = lax.rem(me, 2)
    mate, far = me + 1 - 2 * odd, me - 1 + 2 * odd
    has_far = jnp.logical_and(far >= 0, far < count // 2)
    other = 1 - sec
    order = (1 - odd, odd)

    loads = [
        pltpu.make_async_copy(source, target, load_sem.at[n])
        for n, (source, target) in enumerate((
            (strength_hbm, strength), (shift_hbm, shift), (onsite_hbm, onsite),
            (hop_hbm.at[0], hop), (ham_hbm.at[0], ham), (green_hbm.at[:, 0], green)))
    ]
    for load in loads:
        load.start()

    barrier = pltpu.get_barrier_semaphore()
    pl.semaphore_signal(barrier, inc=1, device_id=(me, other), device_id_type=MESH)
    pl.semaphore_signal(barrier, inc=1, device_id=(mate, sec), device_id_type=MESH)

    @pl.when(has_far)
    def _():
        pl.semaphore_signal(barrier, inc=1, device_id=(far, sec), device_id_type=MESH)

    pl.semaphore_wait(barrier, 2 + has_far.astype(jnp.int32))

    def cut(c):
        return pl.ds(c * rows, rows)

    def to_far(j, c):
        source = odd if j == 0 else 1 - odd
        n = j * CHUNKS + c
        return pltpu.make_async_remote_copy(
            green_hbm.at[source, 0, :, cut(c)], far_buf.at[j, :, cut(c)], far_send.at[n],
            far_recv.at[n], device_id=(far, sec), device_id_type=MESH)

    def to_mate(j):
        source = 1 - odd if j == 0 else odd
        return pltpu.make_async_remote_copy(
            green_hbm.at[source, 0], mate_buf.at[j], mate_send.at[j], mate_recv.at[j],
            device_id=(mate, sec), device_id_type=MESH)

    def swap(j, c, slab):
        n = j * CHUNKS + c
        return pltpu.make_async_remote_copy(
            mat.at[slab, j, :, cut(c)], mat.at[slab, j, :, cut(c)], mat_send.at[n],
            mat_recv.at[n], device_id=(me, other), device_id_type=MESH)

    def site_copy(slab):
        return pltpu.make_async_remote_copy(
            site.at[slab], site.at[slab], small_send.at[0], small_recv.at[0],
            device_id=(me, other), device_id_type=MESH)

    def link_down():
        return pltpu.make_async_remote_copy(
            hop_hbm.at[0, odd], link.at[odd], small_send.at[1], small_recv.at[1],
            device_id=(me, other), device_id_type=MESH)

    def link_across(part):
        return pltpu.make_async_remote_copy(
            link.at[part], link.at[part], small_send.at[2], small_recv.at[2],
            device_id=(mate, sec), device_id_type=MESH)

    pl.when(sec == 1)(lambda: link_down().start())

    @pl.when(has_far)
    def _():
        for c in range(CHUNKS):
            to_far(0, c).start()

    to_mate(0).start()
    to_mate(1).start()

    @pl.when(has_far)
    def _():
        for c in range(CHUNKS):
            to_far(1, c).start()

    @pl.when(jnp.logical_not(has_far))
    def _():
        far_buf[...] = jnp.zeros(far_buf.shape, jnp.float32)

    for load in loads:
        load.wait()
    site[sec] = jnp.broadcast_to(onsite[...], (8, norb))
    site_copy(sec).start()

    eye = lax.broadcasted_iota(jnp.int32, (norb, norb), 0) == lax.broadcasted_iota(
        jnp.int32, (norb, norb), 1)
    w1, w2 = jnp.float32(0.0), jnp.float32(0.0)
    for m in range(strength.shape[0]):
        w1 = w1 + jnp.where(shift[m] == 1, strength[m], 0.0)
        w2 = w2 + jnp.where(shift[m] == 2, strength[m], 0.0)

    def energy(k):
        return -1.5 + 3.0 * ((2 * me + k).astype(jnp.float32) + 0.5) / count

    local[0] = 0.5 * (ham[0] + ham[0].T) + jnp.where(eye, onsite[...], 0.0)
    local[1] = 0.5 * (ham[1] - ham[1].T) - jnp.where(eye, ETA, 0.0)

    @pl.when(sec == 0)
    def _():
        block = hop[0], hop[1]
        real, imag = cmul_split(adj(block), block)
        local[0] = local[0] + LEAD * imag
        local[1] = local[1] - LEAD * real

    @pl.when(sec == 1)
    def _():
        link[...] = hop[...]
        link_h[0], link_h[1] = adj((hop[0], hop[1]))

    to_mate(0).wait_recv()
    to_mate(1).wait_recv()

    def assemble(j, c):
        pl.when(has_far)(lambda: to_far(j, c).wait_recv())
        r = slice(c * rows, (c + 1) * rows)
        for part in range(2):
            near, here = far_buf[0, part, r], green[1 - order[j], part, r]
            if j == 0:
                sigma = w1 * (here + mate_buf[0, part, r]) + w2 * (near + mate_buf[1, part, r])
            else:
                sigma = w1 * (here + near) + w2 * (far_buf[1, part, r] + mate_buf[0, part, r])
            value = -local[part, r] - sigma
            if part == 0:
                value = value + jnp.where(eye[r], energy(order[j]), 0.0)
            mat[sec, j, part, r] = value
        swap(j, c, sec).start()

    def newton(matrix, slab, k):
        row = energy(k) - site[slab][:1]
        col = jnp.sum(jnp.where(eye, row, 0.0), axis=1, keepdims=True)
        rre = row / (row * row + ETA * ETA)
        rim = -ETA / (row * row + ETA * ETA)
        cre = col / (col * col + ETA * ETA)
        cim = -ETA / (col * col + ETA * ETA)
        wre, wim = cre * rre - cim * rim, cre * rim + cim * rre
        xre = jnp.where(eye, 2.0 * rre, 0.0) - (matrix[0] * wre - matrix[1] * wim)
        xim = jnp.where(eye, 2.0 * rim, 0.0) - (matrix[0] * wim + matrix[1] * wre)
        guess = xre, xim
        again = cmul_split(guess, cmul_split(matrix, guess))
        return 2.0 * xre - again[0], 2.0 * xim - again[1]

    def arrived(j, slab):
        for c in range(CHUNKS):
            swap(j, c, slab).wait_recv()

    def first_slab(j):
        g = newton((mat[0, j, 0], mat[0, j, 1]), 0, order[j])
        left[0], left[1] = g

    def couple():
        half = cmul_split((link_h[0], link_h[1]), (left[0], left[1]))
        coup[0], coup[1] = cmul_split(half, (link[0], link[1]))

    def store(j):
        return pltpu.make_async_copy(result.at[j], out_hbm.at[order[j], 0], out_sem.at[j])

    def second_slab(j):
        pl.when(sec == 0)(lambda: arrived(j, 1))
        g1 = newton((mat[1, j, 0] - coup[0], mat[1, j, 1] - coup[1]), 1, order[j])
        result[j, 0], result[j, 1] = g1

        @pl.when(sec == 0)
        def _():
            g1 = result[j, 0], result[j, 1]
            g0 = left[0], left[1]
            half = cmul_split((link[0], link[1]), g1)
            right = cmul_split(half, (link_h[0], link_h[1]))
            more = cmul_split(g0, cmul_split(right, g0))
            result[j, 0] = g0[0] + more[0]
            result[j, 1] = g0[1] + more[1]

        store(j).start()

    for c in range(CHUNKS):
        assemble(0, c)

    @pl.when(sec == 0)
    def _():
        link_down().wait_recv()
        link_across(odd).start()
        site_copy(1).wait_recv()
        first_slab(0)

    assemble(1, 0)

    @pl.when(sec == 0)
    def _():
        link_across(1 - odd).wait_recv()
        link_h[0], link_h[1] = adj((link[0], link[1]))

    @pl.when(sec == 1)
    def _():
        site_copy(0).wait_recv()
        arrived(0, 0)
        first_slab(0)

    couple()
    for c in range(1, CHUNKS - 1):
        assemble(1, c)
    second_slab(0)
    assemble(1, CHUNKS - 1)
    pl.when(sec == 1)(lambda: arrived(1, 0))
    first_slab(1)
    couple()
    second_slab(1)

    for j in range(2):
        for c in range(CHUNKS):
            pl.when(has_far)(lambda j=j, c=c: to_far(j, c).wait_send())
            swap(j, c, sec).wait_send()
        to_mate(j).wait_send()
        store(j).wait()
    site_copy(sec).wait_send()
    pl.when(sec == 1)(lambda: link_down().wait_send())
    pl.when(sec == 0)(lambda: link_across(odd).wait_send())


def two_slabs(green_prev, slab_ham, onsite, hop, mode_strength, phonon_shift):
    norb = green_prev.shape[3]
    count = green_prev.shape[0] * lax.axis_size("energy")
    hbm = pl.BlockSpec(memory_space=pltpu.HBM)
    one = pltpu.VMEM((2, norb, norb), jnp.float32)
    pair = pltpu.VMEM((2, 2, norb, norb), jnp.float32)
    sems = lambda n: pltpu.SemaphoreType.DMA((n,))
    return pl.pallas_call(
        partial(wire_kernel, count),
        out_shape=jax.ShapeDtypeStruct(green_prev.shape, jnp.float32),
        in_specs=[hbm] * 6,
        out_specs=hbm,
        scratch_shapes=[
            pltpu.SMEM(mode_strength.shape, jnp.float32),
            pltpu.SMEM(phonon_shift.shape, jnp.int32),
            pair, one, pltpu.VMEM(onsite.shape, jnp.float32), one,
            pair, pair, one,
            pltpu.VMEM((2, 2, 2, norb, norb), jnp.float32),
            one, one,
            pltpu.VMEM((2, 8, norb), jnp.float32),
            one, one, pair,
            sems(6), sems(2 * CHUNKS), sems(2 * CHUNKS), sems(2), sems(2),
            sems(2 * CHUNKS), sems(2 * CHUNKS), sems(3), sems(3), sems(2),
        ],
        compiler_params=pltpu.CompilerParams(
            collective_id=0, has_side_effects=True, vmem_limit_bytes=63 * 1024 * 1024),
        name="wire",
    )(mode_strength, phonon_shift, green_prev, slab_ham, onsite, hop)


def solution(mesh):
    return jax.shard_map(
        two_slabs if mesh.shape["section"] == 2 and mesh.shape["energy"] % 2 == 0 else body,
        mesh=mesh,
        in_specs=(
            P("energy", "section", None, None, None),
            P("section", None, None, None),
            P("section", None),
            P("section", None, None, None),
            P(),
            P(),
        ),
        out_specs=P("energy", "section", None, None, None),
        check_vma=False,
    )
```

```python
from functools import partial

import jax
import jax.numpy as jnp
from jax import lax
from jax.experimental import pallas as pl
from jax.experimental.pallas import tpu as pltpu
from jax.sharding import PartitionSpec as P

ETA = 1.0
LEAD = 0.5


def extended(block, sides, width):
    for axis, dim in sides:
        count = lax.axis_size(axis)
        forward = [(i, i + 1) for i in range(count - 1)]
        backward = [(target, source) for source, target in forward]
        low = lax.ppermute(
            lax.slice_in_dim(block, block.shape[dim] - width, None, axis=dim), axis, forward
        )
        high = lax.ppermute(lax.slice_in_dim(block, 0, width, axis=dim), axis, backward)
        block = jnp.concatenate([low, block, high], axis=dim)
    return block


def shifted(array, axis, by):
    count = lax.axis_size(axis)
    pairs = [(i, i + by) for i in range(count) if 0 <= i + by < count]
    return lax.ppermute(array, axis, pairs)


def cmul(left_op, right_op):
    matmul = partial(jnp.matmul, precision=lax.Precision.HIGHEST)
    lre, lim = (left_op[..., 0, :, :], left_op[..., 1, :, :])
    rre, rim = (right_op[..., 0, :, :], right_op[..., 1, :, :])
    return jnp.stack(
        [matmul(lre, rre) - matmul(lim, rim), matmul(lre, rim) + matmul(lim, rre)], axis=-3
    )


def adjoint(block):
    return jnp.stack(
        [jnp.swapaxes(block[..., 0, :, :], -1, -2), -jnp.swapaxes(block[..., 1, :, :], -1, -2)],
        axis=-3,
    )


def left_connected(left, energies, sigma, ham, site, link, eye):
    couple = cmul(cmul(adjoint(link), left), link)
    real_part = energies[:, None, None] * eye[None]
    imag_part = ETA * eye[None]
    matrix = jnp.stack([real_part, imag_part], axis=1) - ham[None] - sigma - couple
    offset = energies[:, None] - site[None, :]
    denom = offset * offset + ETA * ETA
    guess = jnp.stack(
        [eye[None] * (offset / denom)[:, None, :], eye[None] * (-ETA / denom)[:, None, :]], axis=1
    )
    for sweep_step in range(2):
        guess = 2.0 * guess - cmul(guess, cmul(matrix, guess))
    return guess


def full_and_message(left, message, link):
    full = left + cmul(left, cmul(message, left))
    return (full, cmul(cmul(link, full), adjoint(link)))


def body(green_prev, slab_ham, onsite, hop, mode_strength, phonon_shift):
    ne_dev = green_prev.shape[0]
    norb = green_prev.shape[3]
    eye = jnp.eye(norb, dtype=jnp.float32)
    padded = extended(green_prev, (("energy", 0),), ne_dev)
    sigma = jnp.zeros((ne_dev, 2, norb, norb), jnp.float32)
    for mode in range(mode_strength.shape[0]):
        shift = phonon_shift[mode]
        lower = lax.dynamic_slice_in_dim(padded, ne_dev - shift, ne_dev, 0)
        upper = lax.dynamic_slice_in_dim(padded, ne_dev + shift, ne_dev, 0)
        sigma = sigma + mode_strength[mode] * (lower[:, 0] + upper[:, 0])
    count = ne_dev * lax.axis_size("energy")
    first = lax.axis_index("energy") * ne_dev
    energies = (
        -1.5
        + 3.0 * ((first + jnp.arange(ne_dev, dtype=jnp.int32)).astype(jnp.float32) + 0.5) / count
    )
    site = onsite[0]
    block = slab_ham[0]
    herm = 0.5 * (block + adjoint(block))
    ham = jnp.stack([herm[0] + eye * site[None, :], herm[1]])
    link = hop[0]
    section = lax.axis_index("section")
    nsec = lax.axis_size("section")
    zero_block = jnp.zeros((norb, norb), jnp.float32)
    lead_one = jnp.stack([zero_block, -LEAD * eye])[None]
    empty_one = jnp.zeros((1, 2, norb, norb), jnp.float32)
    empty_all = jnp.zeros((ne_dev, 2, norb, norb), jnp.float32)

    def forward_turn(turn, carry):
        received, stored = carry
        slot = turn - section
        active = (slot >= 0) & (slot < ne_dev)
        pick = jnp.clip(slot, 0, ne_dev - 1)
        left = jnp.where(section == 0, lead_one, received)
        energy_one = lax.dynamic_slice_in_dim(energies, pick, 1, 0)
        sigma_one = lax.dynamic_slice_in_dim(sigma, pick, 1, 0)
        result = lax.cond(
            active,
            lambda: left_connected(left, energy_one, sigma_one, ham, site, link, eye),
            lambda: empty_one,
        )
        stored = jnp.where(active, lax.dynamic_update_slice_in_dim(stored, result, pick, 0), stored)
        received = shifted(result, "section", 1)
        return (received, stored)

    unused, lefts = lax.fori_loop(0, nsec + ne_dev - 1, forward_turn, (empty_one, empty_all))

    def backward_turn(turn, carry):
        received, stored = carry
        slot = turn - (nsec - 1 - section)
        active = (slot >= 0) & (slot < ne_dev)
        pick = jnp.clip(slot, 0, ne_dev - 1)
        message = jnp.where(section == nsec - 1, empty_one, received)
        left_one = lax.dynamic_slice_in_dim(lefts, pick, 1, 0)
        full, sent = lax.cond(
            active,
            lambda: full_and_message(left_one, message, link),
            lambda: (empty_one, empty_one),
        )
        stored = jnp.where(active, lax.dynamic_update_slice_in_dim(stored, full, pick, 0), stored)
        received = shifted(sent, "section", -1)
        return (received, stored)

    unused, fulls = lax.fori_loop(0, nsec + ne_dev - 1, backward_turn, (empty_one, empty_all))
    return fulls[:, None]


MESH = pl.DeviceIdType.MESH
CHUNKS = 8


def split(value):
    high = value.astype(jnp.bfloat16)
    low = (value - high.astype(jnp.float32)).astype(jnp.bfloat16)
    return high, low


def product(a, b):
    (ah, al), (bh, bl) = a, b
    return jnp.dot(
        jnp.concatenate([ah, al, ah], axis=1), jnp.concatenate([bh, bh, bl], axis=0),
        preferred_element_type=jnp.float32)


def cmul_split(a, b):
    rere = product(split(a[0]), split(b[0]))
    imim = product(split(a[1]), split(b[1]))
    mixed = product(split(a[0] + a[1]), split(b[0] + b[1]))
    return rere - imim, mixed - rere - imim


def adj(block):
    return block[0].T, -block[1].T


def wire_kernel(
    count, strength_hbm, shift_hbm, green_hbm, ham_hbm, onsite_hbm, hop_hbm, out_hbm,
    strength, shift, green, ham, onsite, hop, far_buf, mate_buf, local, mat, link, link_h, site,
    coup, left, result,
    load_sem, far_send, far_recv, mate_send, mate_recv, mat_send, mat_recv, small_send, small_recv,
    out_sem,
):
    me, sec = lax.axis_index("energy"), lax.axis_index("section")
    norb = green.shape[-1]
    rows = norb // CHUNKS
    odd = lax.rem(me, 2)
    mate, far = me + 1 - 2 * odd, me - 1 + 2 * odd
    has_far = jnp.logical_and(far >= 0, far < count // 2)
    other = 1 - sec
    order = (1 - odd, odd)

    loads = [
        pltpu.make_async_copy(source, target, load_sem.at[n])
        for n, (source, target) in enumerate((
            (strength_hbm, strength), (shift_hbm, shift), (onsite_hbm, onsite),
            (hop_hbm.at[0], hop), (ham_hbm.at[0], ham), (green_hbm.at[:, 0], green)))
    ]
    for load in loads:
        load.start()

    barrier = pltpu.get_barrier_semaphore()
    pl.semaphore_signal(barrier, inc=1, device_id=(me, other), device_id_type=MESH)
    pl.semaphore_signal(barrier, inc=1, device_id=(mate, sec), device_id_type=MESH)

    @pl.when(has_far)
    def _():
        pl.semaphore_signal(barrier, inc=1, device_id=(far, sec), device_id_type=MESH)

    pl.semaphore_wait(barrier, 2 + has_far.astype(jnp.int32))

    def cut(c):
        return pl.ds(c * rows, rows)

    def to_far(j, c):
        source = odd if j == 0 else 1 - odd
        n = j * CHUNKS + c
        return pltpu.make_async_remote_copy(
            green_hbm.at[source, 0, :, cut(c)], far_buf.at[j, :, cut(c)], far_send.at[n],
            far_recv.at[n], device_id=(far, sec), device_id_type=MESH)

    def to_mate(j):
        source = 1 - odd if j == 0 else odd
        return pltpu.make_async_remote_copy(
            green_hbm.at[source, 0], mate_buf.at[j], mate_send.at[j], mate_recv.at[j],
            device_id=(mate, sec), device_id_type=MESH)

    def swap(j, c, slab):
        n = j * CHUNKS + c
        return pltpu.make_async_remote_copy(
            mat.at[slab, j, :, cut(c)], mat.at[slab, j, :, cut(c)], mat_send.at[n],
            mat_recv.at[n], device_id=(me, other), device_id_type=MESH)

    def site_copy(slab):
        return pltpu.make_async_remote_copy(
            site.at[slab], site.at[slab], small_send.at[0], small_recv.at[0],
            device_id=(me, other), device_id_type=MESH)

    def link_down():
        return pltpu.make_async_remote_copy(
            hop_hbm.at[0, odd], link.at[odd], small_send.at[1], small_recv.at[1],
            device_id=(me, other), device_id_type=MESH)

    def link_across(part):
        return pltpu.make_async_remote_copy(
            link.at[part], link.at[part], small_send.at[2], small_recv.at[2],
            device_id=(mate, sec), device_id_type=MESH)

    pl.when(sec == 1)(lambda: link_down().start())

    @pl.when(has_far)
    def _():
        for c in range(CHUNKS):
            to_far(0, c).start()

    to_mate(0).start()
    to_mate(1).start()

    @pl.when(has_far)
    def _():
        for c in range(CHUNKS):
            to_far(1, c).start()

    @pl.when(jnp.logical_not(has_far))
    def _():
        far_buf[...] = jnp.zeros(far_buf.shape, jnp.float32)

    for load in loads:
        load.wait()
    site[sec] = jnp.broadcast_to(onsite[...], (8, norb))
    site_copy(sec).start()

    eye = lax.broadcasted_iota(jnp.int32, (norb, norb), 0) == lax.broadcasted_iota(
        jnp.int32, (norb, norb), 1)
    w1, w2 = jnp.float32(0.0), jnp.float32(0.0)
    for m in range(strength.shape[0]):
        w1 = w1 + jnp.where(shift[m] == 1, strength[m], 0.0)
        w2 = w2 + jnp.where(shift[m] == 2, strength[m], 0.0)

    def energy(k):
        return -1.5 + 3.0 * ((2 * me + k).astype(jnp.float32) + 0.5) / count

    local[0] = 0.5 * (ham[0] + ham[0].T) + jnp.where(eye, onsite[...], 0.0)
    local[1] = 0.5 * (ham[1] - ham[1].T) - jnp.where(eye, ETA, 0.0)

    @pl.when(sec == 0)
    def _():
        block = hop[0], hop[1]
        real, imag = cmul_split(adj(block), block)
        local[0] = local[0] + LEAD * imag
        local[1] = local[1] - LEAD * real

    @pl.when(sec == 1)
    def _():
        link[...] = hop[...]
        link_h[0], link_h[1] = adj((hop[0], hop[1]))

    to_mate(0).wait_recv()
    to_mate(1).wait_recv()

    def assemble(j, c):
        pl.when(has_far)(lambda: to_far(j, c).wait_recv())
        r = slice(c * rows, (c + 1) * rows)
        for part in range(2):
            near, here = far_buf[0, part, r], green[1 - order[j], part, r]
            if j == 0:
                sigma = w1 * (here + mate_buf[0, part, r]) + w2 * (near + mate_buf[1, part, r])
            else:
                sigma = w1 * (here + near) + w2 * (far_buf[1, part, r] + mate_buf[0, part, r])
            value = -local[part, r] - sigma
            if part == 0:
                value = value + jnp.where(eye[r], energy(order[j]), 0.0)
            mat[sec, j, part, r] = value
        swap(j, c, sec).start()

    def newton(matrix, slab, k):
        row = energy(k) - site[slab][:1]
        col = jnp.sum(jnp.where(eye, row, 0.0), axis=1, keepdims=True)
        rre = row / (row * row + ETA * ETA)
        rim = -ETA / (row * row + ETA * ETA)
        cre = col / (col * col + ETA * ETA)
        cim = -ETA / (col * col + ETA * ETA)
        wre, wim = cre * rre - cim * rim, cre * rim + cim * rre
        xre = jnp.where(eye, 2.0 * rre, 0.0) - (matrix[0] * wre - matrix[1] * wim)
        xim = jnp.where(eye, 2.0 * rim, 0.0) - (matrix[0] * wim + matrix[1] * wre)
        guess = xre, xim
        again = cmul_split(guess, cmul_split(matrix, guess))
        return 2.0 * xre - again[0], 2.0 * xim - again[1]

    def arrived(j, slab):
        for c in range(CHUNKS):
            swap(j, c, slab).wait_recv()

    def first_slab(j):
        g = newton((mat[0, j, 0], mat[0, j, 1]), 0, order[j])
        left[0], left[1] = g

    def couple():
        half = cmul_split((link_h[0], link_h[1]), (left[0], left[1]))
        coup[0], coup[1] = cmul_split(half, (link[0], link[1]))

    def store(j):
        return pltpu.make_async_copy(result.at[j], out_hbm.at[order[j], 0], out_sem.at[j])

    def second_slab(j):
        pl.when(sec == 0)(lambda: arrived(j, 1))
        g1 = newton((mat[1, j, 0] - coup[0], mat[1, j, 1] - coup[1]), 1, order[j])
        result[j, 0], result[j, 1] = g1

        @pl.when(sec == 0)
        def _():
            g1 = result[j, 0], result[j, 1]
            g0 = left[0], left[1]
            half = cmul_split((link[0], link[1]), g1)
            right = cmul_split(half, (link_h[0], link_h[1]))
            more = cmul_split(g0, cmul_split(right, g0))
            result[j, 0] = g0[0] + more[0]
            result[j, 1] = g0[1] + more[1]

        store(j).start()

    for c in range(CHUNKS):
        assemble(0, c)

    @pl.when(sec == 0)
    def _():
        link_down().wait_recv()
        link_across(odd).start()
        site_copy(1).wait_recv()
        first_slab(0)

    for c in range(CHUNKS // 4):
        assemble(1, c)

    @pl.when(sec == 0)
    def _():
        link_across(1 - odd).wait_recv()
        link_h[0], link_h[1] = adj((link[0], link[1]))

    @pl.when(sec == 1)
    def _():
        site_copy(0).wait_recv()
        arrived(0, 0)
        first_slab(0)

    couple()
    for c in range(CHUNKS // 4, CHUNKS * 3 // 4):
        assemble(1, c)
    second_slab(0)
    for c in range(CHUNKS * 3 // 4, CHUNKS):
        assemble(1, c)
    pl.when(sec == 1)(lambda: arrived(1, 0))
    first_slab(1)
    couple()
    second_slab(1)

    for j in range(2):
        for c in range(CHUNKS):
            pl.when(has_far)(lambda j=j, c=c: to_far(j, c).wait_send())
            swap(j, c, sec).wait_send()
        to_mate(j).wait_send()
        store(j).wait()
    site_copy(sec).wait_send()
    pl.when(sec == 1)(lambda: link_down().wait_send())
    pl.when(sec == 0)(lambda: link_across(odd).wait_send())


def two_slabs(green_prev, slab_ham, onsite, hop, mode_strength, phonon_shift):
    norb = green_prev.shape[3]
    count = green_prev.shape[0] * lax.axis_size("energy")
    hbm = pl.BlockSpec(memory_space=pltpu.HBM)
    one = pltpu.VMEM((2, norb, norb), jnp.float32)
    pair = pltpu.VMEM((2, 2, norb, norb), jnp.float32)
    sems = lambda n: pltpu.SemaphoreType.DMA((n,))
    return pl.pallas_call(
        partial(wire_kernel, count),
        out_shape=jax.ShapeDtypeStruct(green_prev.shape, jnp.float32),
        in_specs=[hbm] * 6,
        out_specs=hbm,
        scratch_shapes=[
            pltpu.SMEM(mode_strength.shape, jnp.float32),
            pltpu.SMEM(phonon_shift.shape, jnp.int32),
            pair, one, pltpu.VMEM(onsite.shape, jnp.float32), one,
            pair, pair, one,
            pltpu.VMEM((2, 2, 2, norb, norb), jnp.float32),
            one, one,
            pltpu.VMEM((2, 8, norb), jnp.float32),
            one, one, pair,
            sems(6), sems(2 * CHUNKS), sems(2 * CHUNKS), sems(2), sems(2),
            sems(2 * CHUNKS), sems(2 * CHUNKS), sems(3), sems(3), sems(2),
        ],
        compiler_params=pltpu.CompilerParams(
            collective_id=0, has_side_effects=True, vmem_limit_bytes=63 * 1024 * 1024),
        name="wire",
    )(mode_strength, phonon_shift, green_prev, slab_ham, onsite, hop)


def solution(mesh):
    return jax.shard_map(
        two_slabs if mesh.shape["section"] == 2 and mesh.shape["energy"] % 2 == 0 else body,
        mesh=mesh,
        in_specs=(
            P("energy", "section", None, None, None),
            P("section", None, None, None),
            P("section", None),
            P("section", None, None, None),
            P(),
            P(),
        ),
        out_specs=P("energy", "section", None, None, None),
        check_vma=False,
    )
```
